32 devices in a mesh: wide: 8 (over z, x), narrow: 4 (over y, core).
Axes of the slice: x: 2, y: 2, z: 4, core: 2. Of those that a mesh axis runs over, the one named last changes fastest.
Arguments:
- sigma_irr: float32 [224, 2, 2, 1600], P('wide'), may hold values from -6 to 6
- star_irr: int32 [8, 8, 32], P('wide', 'narrow'), may hold values from 0 to 223, as said below
- star_sym: int32 [8, 8, 32], P('wide', 'narrow'), may hold values from 0 to 47
- rep_matrices: float32 [48, 40, 40], replicated, may hold values from -1 to 1
Outputs:
- sigma_lattice: float32 [8, 8, 32, 2, 2, 1600], P('narrow', None, 'wide')
The draws below stay inside these ranges and needn't reach their ends.
Inputs may be any that keep to these rules, and one draw needn't show every extreme that they name: Among the 1 x 2 x 32 mesh points of one device, at most 16 have an irreducible point held by one owner (star_irr // 28); on every device some owner is named exactly 16 times.
All inputs are finite; a program needn't handle non-finite values.
Results may differ from the reference program's by a relative error of at most 0.00007.
Values sent between devices are 32-bit elements; how exact they have to be, the bound alone decides.
A program may use at most 64 MiB of HBM per device.

```python
import jax
import jax.numpy as jnp
from jax import lax

W = 40
FREQ = 2
NSYM = 48
NKZ = 32
KX_DEV = 1
KY_DEV = 2
IRR_DEV = 28
NKX = 8
NKY = 8
NIRR = 224


def draw_star_irr(key, part):
    key = jax.random.fold_in(key, 11)
    owners_count = NKX // KX_DEV
    rows_count = NKY // KY_DEV
    points = KX_DEV * KY_DEV * NKZ
    capacity = 2 * points // owners_count
    slot_index = jnp.arange(points, dtype=jnp.int32)
    group_index = slot_index // (2 * capacity)
    within_group = slot_index % (2 * capacity)
    owner_rank = 4 * group_index + (within_group >= capacity).astype(jnp.int32)
    owner_rank = owner_rank + (within_group >= capacity + capacity // 2).astype(jnp.int32)
    owner_rank = owner_rank + (within_group >= capacity + 3 * capacity // 4).astype(jnp.int32)
    device_keys = jax.random.split(key, owners_count * rows_count)

    def one_device(device_key):
        key_map, key_order, key_local = jax.random.split(device_key, 3)
        mapping = jax.random.permutation(key_map, owners_count)
        shuffle = jax.random.permutation(key_order, points)
        owner_id = mapping[owner_rank][shuffle]
        local_row = jax.random.randint(key_local, (points,), 0, IRR_DEV)
        return (owner_id * IRR_DEV + local_row).astype(jnp.int32)
    star_table = jax.vmap(one_device)(device_keys)
    star_table = star_table.reshape(owners_count, rows_count, KX_DEV, KY_DEV, NKZ)
    star_table = star_table.transpose(0, 2, 1, 3, 4).reshape(NKX, NKY, NKZ)
    return star_table.astype(jnp.int32)


def touch_ends(result, own_key, smallest, high):
    extent = result.shape
    index_at = [jax.random.randint(jax.random.fold_in(own_key, axis), (), 0, extent[axis]) for axis in range(len(extent))]
    result = result.at[tuple(index_at)].set(smallest)
    longest = extent.index(max(extent))
    index_at[longest] = (index_at[longest] + 1) % extent[longest]
    return result.at[tuple(index_at)].set(high)


def levels(own_key, shape, pieces, low, largest):
    factor_of = 1.0
    for axis_at, blocks in pieces:
        heights = jax.random.uniform(jax.random.fold_in(jax.random.fold_in(own_key, 6), axis_at), (blocks,), jnp.float32, low / len(pieces), largest / len(pieces))
        factor_of = factor_of * jnp.repeat(jnp.exp(heights), shape[axis_at] // blocks).reshape((-1,) + (1,) * (len(shape) - 1 - axis_at))
    return factor_of


def gaussian(key, extent, spread, limit, cuts=(), held_as=jnp.bfloat16):
    values = spread * jax.random.normal(key, extent, jnp.float32)
    if cuts:
        values = values * levels(key, extent, cuts, -0.22, 0.18)
    return jnp.clip(values, -limit, limit).astype(held_as)


def setup_inputs(seed: int = 0) -> dict:
    arg_keys = jax.random.split(jax.random.key(seed), 5)
    return {
        "sigma_irr": gaussian(arg_keys[0], (NIRR, FREQ, 2, W * W), 1.0, 6.0, ((0, 8),), jnp.float32),
        "star_irr": draw_star_irr(jax.random.fold_in(arg_keys[4], 71), 0),
        "star_sym": touch_ends(jax.random.randint(arg_keys[2], (NKX, NKY, NKZ), 0, NSYM), jax.random.fold_in(arg_keys[2], 1), 0, NSYM - 1).astype(jnp.int32),
        "rep_matrices": gaussian(arg_keys[3], (NSYM, W, W), W ** -0.5, 1.0, (), jnp.float32),
    }


def reference(sigma_irr, star_irr, star_sym, rep_matrices):
    orbitals = rep_matrices.shape[1]

    def one_frequency(freq_index):
        chosen_freq = jnp.take(sigma_irr, freq_index, axis=1)

        def unfold_plane(plane_pair):
            irr_plane, sym_plane = plane_pair
            blocks = chosen_freq[irr_plane]
            square = blocks.reshape(blocks.shape[:3] + (orbitals, orbitals))
            rotation = rep_matrices[sym_plane]
            partial_product = jnp.einsum("yzab,yzcbd->yzcad", rotation, square, precision=lax.Precision.HIGHEST)
            turned = jnp.einsum("yzcad,yzed->yzcae", partial_product, rotation, precision=lax.Precision.HIGHEST)
            return turned.reshape(blocks.shape)

        unfolded = lax.map(unfold_plane, (star_irr, star_sym))
        spectrum = jnp.fft.fftn(unfolded[:, :, :, 0] + 1j * unfolded[:, :, :, 1], axes=(0, 1, 2), norm="ortho")
        return jnp.stack([spectrum.real, spectrum.imag], axis=3)

    stacked = lax.map(one_frequency, jnp.arange(FREQ))
    return jnp.moveaxis(stacked, 0, 3)
```

```python
import functools
import math

import jax
import jax.numpy as jnp
from jax import lax
from jax.experimental import pallas as pl
from jax.experimental.pallas import tpu as pltpu
from jax.sharding import PartitionSpec as P

MESH = pl.DeviceIdType.MESH
LANES = 128
SUB = 8


def twiddle(value, step, length):
    real, imag = value
    step %= length
    if step == 0:
        return value
    if 4 * step == length:
        return imag, -real
    if 2 * step == length:
        return -real, -imag
    if 8 * step == length:
        root = math.sqrt(0.5)
        return (real + imag) * root, (imag - real) * root
    if 8 * step == 3 * length:
        root = math.sqrt(0.5)
        return (imag - real) * root, -(real + imag) * root
    cosine = math.cos(2 * math.pi * step / length)
    sine = math.sin(2 * math.pi * step / length)
    return real * cosine + imag * sine, imag * cosine - real * sine


def fourier(values):
    length = len(values)
    if length == 1:
        return values
    even = fourier(values[0::2])
    odd = fourier(values[1::2])
    half = length // 2
    odd = [twiddle(odd[i], i, length) for i in range(half)]
    low = [(a[0] + b[0], a[1] + b[1]) for a, b in zip(even, odd)]
    high = [(a[0] - b[0], a[1] - b[1]) for a, b in zip(even, odd)]
    return low + high


def pack(blocks, width):
    total = width * len(blocks)
    tiles = -(-total // LANES)
    lane = lax.broadcasted_iota(jnp.int32, blocks[0].shape, 1)
    made = [None] * tiles
    for index, block in enumerate(blocks):
        tile, offset = divmod(index * width, LANES)
        moved = pltpu.roll(block, offset, 1) if offset else block
        made[tile] = moved if made[tile] is None else jnp.where(lane < offset, made[tile], moved)
        if offset + width > LANES:
            made[tile + 1] = moved
    return made


def unpack(tiles, index, width):
    tile, offset = divmod(index * width, LANES)
    block = tiles[tile]
    if offset + width > LANES:
        lane = lax.broadcasted_iota(jnp.int32, block.shape, 1)
        block = jnp.where(lane >= offset, block, tiles[tile + 1])
    return pltpu.roll(block, LANES - offset, 1) if offset else block


def halves(value):
    high = value.astype(jnp.bfloat16)
    low = (value - high.astype(jnp.float32)).astype(jnp.bfloat16)
    return high, low


def unfold_kernel(
    held, per_tile, orbitals, scale, irr_ref, sym_ref, blocks_ref, right_ref, left_ref, out_ref, unfolded
):
    wide, steps, _, rows_y, _, _ = out_ref.shape
    points = irr_ref.shape[0]
    length = points // rows_y
    lane = lax.broadcasted_iota(jnp.int32, (orbitals, LANES), 1)
    first = lane < orbitals

    def one_point(k, carry):
        irr = irr_ref[k]
        sym = sym_ref[k]
        owner = irr // held
        row = irr - owner * held
        tile = row // per_tile
        shift = (row - tile * per_tile) * orbitals
        block = blocks_ref[owner, :, pl.ds(pl.multiple_of(tile * LANES, LANES), LANES)]
        start = pl.multiple_of((per_tile - 1) * orbitals - shift, SUB)
        weights = right_ref[sym, pl.ds(start, LANES), :]
        high, low = halves(weights)
        block_high, block_low = halves(block)
        product = jnp.dot(
            jnp.concatenate([block_high, block_low], axis=1),
            jnp.concatenate(
                [
                    jnp.concatenate([high, low], axis=1),
                    jnp.concatenate([high, jnp.zeros_like(low)], axis=1),
                ],
                axis=0,
            ),
            preferred_element_type=jnp.float32,
        )
        product = product[:, :LANES] + product[:, LANES:]
        parts = []
        for c in range(2):
            base = 2 * c * orbitals
            parts.append(
                jnp.where(first, product[base : base + orbitals], product[base + orbitals : base + 2 * orbitals])
            )
        half = jnp.concatenate(parts, axis=1)
        half_high = half.astype(jnp.bfloat16).astype(jnp.float32)
        stacked = jnp.concatenate(
            [half_high, half - half_high, half_high, jnp.zeros((LANES - 3 * orbitals, 2 * LANES), jnp.float32)],
            axis=0,
        )
        turned = jnp.dot(
            left_ref[sym].astype(jnp.bfloat16),
            stacked.astype(jnp.bfloat16),
            preferred_element_type=jnp.float32,
        )
        unfolded[0, k] = turned[:, :LANES]
        unfolded[1, k] = turned[:, LANES:]
        return carry

    lax.fori_loop(0, points, one_point, 0, unroll=4)

    per_dest = length // wide

    def one_transform(at, carry):
        y = at // steps
        step = at - y * steps
        rows = pl.ds(pl.multiple_of(step * SUB, SUB), SUB)
        values = [(unfolded[0, y * length + z, rows, :], unfolded[1, y * length + z, rows, :]) for z in range(length)]
        result = fourier(values)
        for dest in range(wide):
            for c in range(2):
                made = pack([result[dest * per_dest + i][c] * scale for i in range(per_dest)], 2 * orbitals)
                for j, tile in enumerate(made):
                    out_ref[dest, step, c, y, j * SUB : (j + 1) * SUB, :] = tile
        return carry

    lax.fori_loop(0, rows_y * steps, one_transform, 0)


def exchange_kernel(
    orbitals, y_ref, out_ref, from_wide, to_narrow, from_narrow, send_wide, recv_wide, send_narrow, recv_narrow, own
):
    wide, steps, _, rows_y, tile_rows, _ = y_ref.shape
    narrow, _, rows_x = to_narrow.shape[:3]
    tiles = tile_rows // SUB
    me_wide = lax.axis_index("wide")
    me_narrow = lax.axis_index("narrow")

    barrier = pltpu.get_barrier_semaphore()
    for i in range(1, wide):
        pl.semaphore_signal(barrier, inc=1, device_id=(lax.rem(me_wide + i, wide), me_narrow), device_id_type=MESH)
    for i in range(1, narrow):
        pl.semaphore_signal(barrier, inc=1, device_id=(me_wide, lax.rem(me_narrow + i, narrow)), device_id_type=MESH)
    pl.semaphore_wait(barrier, wide + narrow - 2)

    def wide_copy(step, i):
        peer = lax.rem(me_wide + i, wide)
        return pltpu.make_async_remote_copy(
            src_ref=y_ref.at[peer, step],
            dst_ref=from_wide.at[me_wide, step],
            send_sem=send_wide.at[step, i],
            recv_sem=recv_wide.at[step, i],
            device_id=(peer, me_narrow),
            device_id_type=MESH,
        )

    def narrow_copy(step, i):
        peer = lax.rem(me_narrow + i, narrow)
        return pltpu.make_async_remote_copy(
            src_ref=to_narrow.at[peer, step],
            dst_ref=from_narrow.at[me_narrow, step],
            send_sem=send_narrow.at[step, i],
            recv_sem=recv_narrow.at[step, i],
            device_id=(me_wide, peer),
            device_id_type=MESH,
        )

    for step in range(steps):
        for i in range(1, wide):
            wide_copy(step, i).start()
    own_copy = pltpu.make_async_copy(y_ref.at[me_wide], from_wide.at[me_wide], own.at[steps])
    own_copy.start()
    own_copy.wait()

    def finish(step):
        for i in range(1, narrow):
            narrow_copy(step, i).wait_recv()
        rows = slice(step * SUB, (step + 1) * SUB)

        def one(x, carry):
            made = []
            for j in range(tiles):
                at = slice(j * SUB, (j + 1) * SUB)
                made.append(
                    fourier(
                        [
                            (from_narrow[n, step, x, 0, y, at, :], from_narrow[n, step, x, 1, y, at, :])
                            for n in range(narrow)
                            for y in range(rows_y)
                        ]
                    )
                )
            for y in range(narrow * rows_y):
                for c in range(2):
                    line = [made[j][y][c] for j in range(tiles)]
                    for z in range(out_ref.shape[2]):
                        for f in range(2):
                            block = unpack(line, 2 * z + f, orbitals)
                            out_ref[x, y, z, f, c, rows, :] = block[:, :orbitals]
            return carry

        lax.fori_loop(0, rows_x, one, 0)

    for step in range(steps):
        for i in range(1, wide):
            wide_copy(step, i).wait_recv()

        def one(at, carry):
            y = at // tiles
            rows = pl.ds(pl.multiple_of((at - y * tiles) * SUB, SUB), SUB)
            values = [
                (from_wide[w, step, 0, y, rows, :], from_wide[w, step, 1, y, rows, :]) for w in range(wide)
            ]
            for x, pair in enumerate(fourier(values)):
                for c in range(2):
                    to_narrow[x // rows_x, step, x % rows_x, c, y, rows, :] = pair[c]
            return carry

        lax.fori_loop(0, rows_y * tiles, one, 0)
        for i in range(1, narrow):
            narrow_copy(step, i).start()
        mine = pltpu.make_async_copy(to_narrow.at[me_narrow, step], from_narrow.at[me_narrow, step], own.at[step])
        mine.start()
        mine.wait()
        if step:
            finish(step - 1)
    finish(steps - 1)
    for step in range(steps):
        for i in range(1, wide):
            wide_copy(step, i).wait_send()
        for i in range(1, narrow):
            narrow_copy(step, i).wait_send()


def spread_blocks(sigma_irr, orbitals, per_tile):
    held, freqs, parts, _ = sigma_irr.shape
    narrow = lax.axis_size("narrow")
    tiles = -(-held // per_tile)
    share = narrow // (freqs * parts)
    if share and orbitals // share % SUB == 0:
        axes = ("wide", "narrow")
        index = lax.axis_index("narrow")
        which, piece = index // share, index % share
        part, freq = which // freqs, which % freqs
        width = orbitals * orbitals // share
        own = lax.dynamic_slice(sigma_irr, (0, freq, part, piece * width), (held, 1, 1, width))
    else:
        axes = "wide"
        own = jnp.swapaxes(sigma_irr, 1, 2)
    own = own.reshape(held, -1, orbitals).transpose(1, 0, 2)
    rows = own.shape[0]
    own = jnp.pad(own, ((0, 0), (0, tiles * per_tile - held), (0, 0)))
    own = own.reshape(rows, tiles, per_tile * orbitals)
    own = jnp.pad(own, ((0, 0), (0, 0), (0, LANES - per_tile * orbitals)))
    own = own.reshape(rows, tiles * LANES)
    every = lax.all_gather(own, axes, axis=0, tiled=True)
    return every.reshape(lax.axis_size("wide"), freqs * parts * orbitals, tiles * LANES)


def local(sigma_irr, star_irr, star_sym, rep_matrices):
    wide, narrow = lax.axis_size("wide"), lax.axis_size("narrow")
    held, freqs, parts, _ = sigma_irr.shape
    orbitals = rep_matrices.shape[1]
    rows_y, length = star_irr.shape[1:]
    per_tile = LANES // orbitals
    per_dest = length // wide
    steps = orbitals // SUB
    tile_rows = SUB * -(-per_dest * freqs * orbitals // LANES)
    size_x, size_y = wide * star_irr.shape[0], narrow * rows_y
    rows_x = size_x // narrow

    blocks = spread_blocks(sigma_irr, orbitals, per_tile)
    turned = jnp.swapaxes(rep_matrices, 1, 2)
    before = (per_tile - 1) * orbitals
    right = jnp.pad(
        jnp.concatenate([turned, turned], axis=2),
        ((0, 0), (before, LANES - orbitals), (0, LANES - 2 * orbitals)),
    )
    high = lax.reduce_precision(rep_matrices, 8, 7)
    left = jnp.pad(
        jnp.concatenate([high, high, rep_matrices - high], axis=2), ((0, 0), (0, 0), (0, LANES - 3 * orbitals))
    )

    vmem = pl.BlockSpec(memory_space=pltpu.VMEM)
    smem = pl.BlockSpec(memory_space=pltpu.SMEM)
    sent = pl.pallas_call(
        functools.partial(
            unfold_kernel, held, per_tile, orbitals, 1.0 / math.sqrt(size_x * size_y * length)
        ),
        out_shape=jax.ShapeDtypeStruct((wide, steps, 2, rows_y, tile_rows, LANES), jnp.float32),
        in_specs=[smem, smem, vmem, vmem, vmem],
        out_specs=vmem,
        scratch_shapes=[pltpu.VMEM((2, rows_y * length, orbitals, LANES), jnp.float32)],
        compiler_params=pltpu.CompilerParams(vmem_limit_bytes=56 * 1024 * 1024),
    )(star_irr.reshape(-1), star_sym.reshape(-1), blocks, right, left)

    slots = (steps, 2, rows_y, tile_rows, LANES)
    middle = (narrow, steps, rows_x, 2, rows_y, tile_rows, LANES)
    result = pl.pallas_call(
        functools.partial(exchange_kernel, orbitals),
        out_shape=jax.ShapeDtypeStruct((rows_x, size_y, per_dest, freqs, 2, orbitals, orbitals), jnp.float32),
        in_specs=[vmem],
        out_specs=vmem,
        scratch_shapes=[
            pltpu.VMEM((wide,) + slots, jnp.float32),
            pltpu.VMEM(middle, jnp.float32),
            pltpu.VMEM(middle, jnp.float32),
            pltpu.SemaphoreType.DMA((steps, wide)),
            pltpu.SemaphoreType.DMA((steps, wide)),
            pltpu.SemaphoreType.DMA((steps, narrow)),
            pltpu.SemaphoreType.DMA((steps, narrow)),
            pltpu.SemaphoreType.DMA((steps + 1,)),
        ],
        compiler_params=pltpu.CompilerParams(
            collective_id=0, has_side_effects=True, vmem_limit_bytes=56 * 1024 * 1024
        ),
    )(sent)
    return result.reshape(result.shape[:5] + (orbitals * orbitals,))


def solution(mesh):
    placed = (
        P("wide", None, None, None),
        P("wide", "narrow", None),
        P("wide", "narrow", None),
        P(),
    )
    return jax.shard_map(
        local,
        mesh=mesh,
        in_specs=placed,
        out_specs=P("narrow", None, "wide", None, None, None),
        check_vma=False,
    )
```

```python
import functools
import math

import jax
import jax.numpy as jnp
from jax import lax
from jax.experimental import pallas as pl
from jax.experimental.pallas import tpu as pltpu
from jax.sharding import PartitionSpec as P

MESH = pl.DeviceIdType.MESH
LANES = 128
SUB = 8


def twiddle(value, step, length):
    real, imag = value
    step %= length
    if step == 0:
        return value
    if 4 * step == length:
        return imag, -real
    if 2 * step == length:
        return -real, -imag
    if 8 * step == length:
        root = math.sqrt(0.5)
        return (real + imag) * root, (imag - real) * root
    if 8 * step == 3 * length:
        root = math.sqrt(0.5)
        return (imag - real) * root, -(real + imag) * root
    cosine = math.cos(2 * math.pi * step / length)
    sine = math.sin(2 * math.pi * step / length)
    return real * cosine + imag * sine, imag * cosine - real * sine


def fourier(values):
    length = len(values)
    if length == 1:
        return values
    even = fourier(values[0::2])
    odd = fourier(values[1::2])
    half = length // 2
    odd = [twiddle(odd[i], i, length) for i in range(half)]
    low = [(a[0] + b[0], a[1] + b[1]) for a, b in zip(even, odd)]
    high = [(a[0] - b[0], a[1] - b[1]) for a, b in zip(even, odd)]
    return low + high


def pack(blocks, width):
    total = width * len(blocks)
    tiles = -(-total // LANES)
    lane = lax.broadcasted_iota(jnp.int32, blocks[0].shape, 1)
    made = [None] * tiles
    for index, block in enumerate(blocks):
        tile, offset = divmod(index * width, LANES)
        moved = pltpu.roll(block, offset, 1) if offset else block
        made[tile] = moved if made[tile] is None else jnp.where(lane < offset, made[tile], moved)
        if offset + width > LANES:
            made[tile + 1] = moved
    return made


def unpack(tiles, index, width):
    tile, offset = divmod(index * width, LANES)
    block = tiles[tile]
    if offset + width > LANES:
        lane = lax.broadcasted_iota(jnp.int32, block.shape, 1)
        block = jnp.where(lane >= offset, block, tiles[tile + 1])
    return pltpu.roll(block, LANES - offset, 1) if offset else block


def halves(value):
    high = value.astype(jnp.bfloat16)
    low = (value - high.astype(jnp.float32)).astype(jnp.bfloat16)
    return high, low


def unfold_kernel(
    held, per_tile, orbitals, scale, irr_ref, sym_ref, blocks_ref, rep_ref, turned_ref, out_ref, unfolded, right_ref, left_ref
):
    wide, steps, _, rows_y, _, _ = out_ref.shape
    length = irr_ref.shape[2]
    points = rows_y * length
    lane = lax.broadcasted_iota(jnp.int32, (orbitals, LANES), 1)
    first = lane < orbitals

    def one_table(sym, carry):
        rep, turned = rep_ref[sym], turned_ref[sym]
        high = rep.astype(jnp.bfloat16).astype(jnp.float32)
        rest = jnp.zeros((orbitals, LANES - 3 * orbitals), jnp.float32)
        left_ref[sym] = jnp.concatenate([high, high, rep - high, rest], axis=1)
        before = (per_tile - 1) * orbitals
        right_ref[sym, 0:before, :] = jnp.zeros((before, LANES), jnp.float32)
        rest = jnp.zeros((orbitals, LANES - 2 * orbitals), jnp.float32)
        right_ref[sym, before : before + orbitals, :] = jnp.concatenate([turned, turned, rest], axis=1)
        right_ref[sym, before + orbitals :, :] = jnp.zeros((LANES - orbitals, LANES), jnp.float32)
        return carry

    lax.fori_loop(0, rep_ref.shape[0], one_table, 0, unroll=2)

    def one_point(k, carry):
        irr = irr_ref[0, k // length, lax.rem(k, length)]
        sym = sym_ref[0, k // length, lax.rem(k, length)]
        owner = irr // held
        row = irr - owner * held
        tile = row // per_tile
        shift = (row - tile * per_tile) * orbitals
        block = blocks_ref[owner, :, pl.ds(pl.multiple_of(tile * LANES, LANES), LANES)]
        start = pl.multiple_of((per_tile - 1) * orbitals - shift, SUB)
        weights = right_ref[sym, pl.ds(start, LANES), :]
        high, low = halves(weights)
        block_high, block_low = halves(block)
        product = jnp.dot(
            jnp.concatenate([block_high, block_low], axis=1),
            jnp.concatenate(
                [
                    jnp.concatenate([high, low], axis=1),
                    jnp.concatenate([high, jnp.zeros_like(low)], axis=1),
                ],
                axis=0,
            ),
            preferred_element_type=jnp.float32,
        )
        product = product[:, :LANES] + product[:, LANES:]
        parts = []
        for c in range(2):
            base = 2 * c * orbitals
            parts.append(
                jnp.where(first, product[base : base + orbitals], product[base + orbitals : base + 2 * orbitals])
            )
        half = jnp.concatenate(parts, axis=1)
        half_high = half.astype(jnp.bfloat16).astype(jnp.float32)
        stacked = jnp.concatenate(
            [half_high, half - half_high, half_high, jnp.zeros((LANES - 3 * orbitals, 2 * LANES), jnp.float32)],
            axis=0,
        )
        turned = jnp.dot(
            left_ref[sym].astype(jnp.bfloat16),
            stacked.astype(jnp.bfloat16),
            preferred_element_type=jnp.float32,
        )
        unfolded[0, k] = turned[:, :LANES]
        unfolded[1, k] = turned[:, LANES:]
        return carry

    lax.fori_loop(0, points, one_point, 0, unroll=4)

    per_dest = length // wide

    def one_transform(at, carry):
        y = at // steps
        step = at - y * steps
        rows = pl.ds(pl.multiple_of(step * SUB, SUB), SUB)
        values = [(unfolded[0, y * length + z, rows, :], unfolded[1, y * length + z, rows, :]) for z in range(length)]
        result = fourier(values)
        for dest in range(wide):
            for c in range(2):
                made = pack([result[dest * per_dest + i][c] * scale for i in range(per_dest)], 2 * orbitals)
                for j, tile in enumerate(made):
                    out_ref[dest, step, c, y, j * SUB : (j + 1) * SUB, :] = tile
        return carry

    lax.fori_loop(0, rows_y * steps, one_transform, 0)


def exchange_kernel(
    orbitals, y_ref, out_ref, from_wide, to_narrow, from_narrow, send_wide, recv_wide, send_narrow, recv_narrow, own
):
    wide, steps, _, rows_y, tile_rows, _ = y_ref.shape
    narrow, _, rows_x = to_narrow.shape[:3]
    tiles = tile_rows // SUB
    me_wide = lax.axis_index("wide")
    me_narrow = lax.axis_index("narrow")

    barrier = pltpu.get_barrier_semaphore()
    for i in range(1, wide):
        pl.semaphore_signal(barrier, inc=1, device_id=(lax.rem(me_wide + i, wide), me_narrow), device_id_type=MESH)
    for i in range(1, narrow):
        pl.semaphore_signal(barrier, inc=1, device_id=(me_wide, lax.rem(me_narrow + i, narrow)), device_id_type=MESH)
    pl.semaphore_wait(barrier, wide + narrow - 2)

    def wide_copy(step, i):
        peer = lax.rem(me_wide + i, wide)
        return pltpu.make_async_remote_copy(
            src_ref=y_ref.at[peer, step],
            dst_ref=from_wide.at[me_wide, step],
            send_sem=send_wide.at[step, i],
            recv_sem=recv_wide.at[step, i],
            device_id=(peer, me_narrow),
            device_id_type=MESH,
        )

    def narrow_copy(step, i):
        peer = lax.rem(me_narrow + i, narrow)
        return pltpu.make_async_remote_copy(
            src_ref=to_narrow.at[peer, step],
            dst_ref=from_narrow.at[me_narrow, step],
            send_sem=send_narrow.at[step, i],
            recv_sem=recv_narrow.at[step, i],
            device_id=(me_wide, peer),
            device_id_type=MESH,
        )

    for step in range(steps):
        for i in range(1, wide):
            wide_copy(step, i).start()
    own_copy = pltpu.make_async_copy(y_ref.at[me_wide], from_wide.at[me_wide], own.at[steps])
    own_copy.start()
    own_copy.wait()

    def finish(step):
        for i in range(1, narrow):
            narrow_copy(step, i).wait_recv()
        rows = slice(step * SUB, (step + 1) * SUB)

        def one(x, carry):
            made = []
            for j in range(tiles):
                at = slice(j * SUB, (j + 1) * SUB)
                made.append(
                    fourier(
                        [
                            (from_narrow[n, step, x, 0, y, at, :], from_narrow[n, step, x, 1, y, at, :])
                            for n in range(narrow)
                            for y in range(rows_y)
                        ]
                    )
                )
            for y in range(narrow * rows_y):
                for c in range(2):
                    line = [made[j][y][c] for j in range(tiles)]
                    for z in range(out_ref.shape[2]):
                        for f in range(2):
                            block = unpack(line, 2 * z + f, orbitals)
                            out_ref[x, y, z, f, c, rows, :] = block[:, :orbitals]
            return carry

        lax.fori_loop(0, rows_x, one, 0)

    for step in range(steps):
        for i in range(1, wide):
            wide_copy(step, i).wait_recv()

        def one(at, carry):
            y = at // tiles
            rows = pl.ds(pl.multiple_of((at - y * tiles) * SUB, SUB), SUB)
            values = [
                (from_wide[w, step, 0, y, rows, :], from_wide[w, step, 1, y, rows, :]) for w in range(wide)
            ]
            for x, pair in enumerate(fourier(values)):
                for c in range(2):
                    to_narrow[x // rows_x, step, x % rows_x, c, y, rows, :] = pair[c]
            return carry

        lax.fori_loop(0, rows_y * tiles, one, 0)
        for i in range(1, narrow):
            narrow_copy(step, i).start()
        mine = pltpu.make_async_copy(to_narrow.at[me_narrow, step], from_narrow.at[me_narrow, step], own.at[step])
        mine.start()
        mine.wait()
        if step:
            finish(step - 1)
    finish(steps - 1)
    for step in range(steps):
        for i in range(1, wide):
            wide_copy(step, i).wait_send()
        for i in range(1, narrow):
            narrow_copy(step, i).wait_send()


def gather_kernel(own_ref, out_ref, send, recv, local_sem):
    depth = out_ref.shape[0] // 2
    wide, narrow = lax.axis_index("wide"), lax.axis_index("narrow")
    z, x = wide // 2, lax.rem(wide, 2)
    y, core = narrow // 2, lax.rem(narrow, 2)
    other_x = z * 2 + 1 - x
    other_y = (1 - y) * 2 + core
    x_peer, y_peer = (other_x, narrow), (wide, other_y)
    core_peer = (wide, y * 2 + 1 - core)
    z_peers = [(lax.rem(z + i, depth) * 2 + x, narrow) for i in range(1, depth)]

    barrier = pltpu.get_barrier_semaphore()
    for peer in z_peers + [x_peer, y_peer, core_peer]:
        pl.semaphore_signal(barrier, inc=1, device_id=peer, device_id_type=MESH)
    pl.semaphore_wait(barrier, depth + 2)

    mine = pltpu.make_async_copy(own_ref, out_ref.at[wide, narrow], local_sem)
    mine.start()
    copies = {}

    def push(name, peer, block):
        at = len(copies)
        source = own_ref if block is None else out_ref.at[block]
        target = (wide, narrow) if block is None else block
        copies[name] = pltpu.make_async_remote_copy(
            src_ref=source,
            dst_ref=out_ref.at[target],
            send_sem=send.at[at],
            recv_sem=recv.at[at],
            device_id=peer,
            device_id_type=MESH,
        )
        copies[name].start()

    def held(j, other_wide, other_narrow):
        source = lax.rem(z + depth - j, depth) * 2 + (1 - x if other_wide else x)
        return source, other_y if other_narrow else narrow

    push("x0", x_peer, None)
    push("y0", y_peer, None)
    for i in range(1, depth):
        push(f"z{i}", z_peers[i - 1], None)
    push("c0", core_peer, None)

    def arrived_z(j):
        copies[f"z{j}"].wait_recv()
        push(f"x{j}", x_peer, held(j, False, False))
        push(f"y{j}", y_peer, held(j, False, False))
        push(f"c{j}", core_peer, held(j, False, False))

    def arrived_xy(j):
        copies[f"x{j}"].wait_recv()
        if 2 * j < depth:
            push(f"yx{j}", y_peer, held(j, True, False))
        push(f"cx{j}", core_peer, held(j, True, False))
        copies[f"y{j}"].wait_recv()
        if 2 * j >= depth:
            push(f"xy{j}", x_peer, held(j, False, True))
        push(f"cy{j}", core_peer, held(j, False, True))

    for j in range(depth):
        if j + 1 < depth:
            arrived_z(j + 1)
        arrived_xy(j)
    for j in range(depth):
        copies[f"yx{j}" if 2 * j < depth else f"xy{j}"].wait_recv()
        push(f"cxy{j}", core_peer, held(j, True, True))
    for name, copy in copies.items():
        if name[0] == "c":
            copy.wait_recv()
    for copy in copies.values():
        copy.wait_send()
    mine.wait()


def gather_blocks(own):
    wide, narrow = lax.axis_size("wide"), lax.axis_size("narrow")
    rows, columns = own.shape
    count = wide * narrow - 1
    vmem = pl.BlockSpec(memory_space=pltpu.VMEM)
    every = pl.pallas_call(
        gather_kernel,
        out_shape=jax.ShapeDtypeStruct((wide, narrow, rows, columns), jnp.float32),
        in_specs=[vmem],
        out_specs=vmem,
        scratch_shapes=[
            pltpu.SemaphoreType.DMA((count,)),
            pltpu.SemaphoreType.DMA((count,)),
            pltpu.SemaphoreType.DMA,
        ],
        compiler_params=pltpu.CompilerParams(
            collective_id=1, has_side_effects=True, vmem_limit_bytes=32 * 1024 * 1024
        ),
    )(own)
    return every.reshape(wide, narrow * rows, columns)


def spread_blocks(sigma_irr, orbitals, per_tile):
    held, freqs, parts, _ = sigma_irr.shape
    narrow = lax.axis_size("narrow")
    tiles = -(-held // per_tile)
    share = narrow // (freqs * parts)
    if share and orbitals // share % SUB == 0:
        axes = ("wide", "narrow")
        index = lax.axis_index("narrow")
        which, piece = index // share, index % share
        part, freq = which // freqs, which % freqs
        width = orbitals * orbitals // share
        own = lax.dynamic_slice(sigma_irr, (0, freq, part, piece * width), (held, 1, 1, width))
    else:
        axes = "wide"
        own = jnp.swapaxes(sigma_irr, 1, 2)
    own = own.reshape(held, -1, orbitals).transpose(1, 0, 2)
    rows = own.shape[0]
    own = jnp.pad(own, ((0, 0), (0, tiles * per_tile - held), (0, 0)))
    own = own.reshape(rows, tiles, per_tile * orbitals)
    own = jnp.pad(own, ((0, 0), (0, 0), (0, LANES - per_tile * orbitals)))
    own = own.reshape(rows, tiles * LANES)
    if (lax.axis_size("wide"), narrow) == (8, 4) and len(axes) == 2:
        return gather_blocks(own)
    every = lax.all_gather(own, axes, axis=0, tiled=True)
    return every.reshape(lax.axis_size("wide"), freqs * parts * orbitals, tiles * LANES)


def local(sigma_irr, star_irr, star_sym, rep_matrices):
    wide, narrow = lax.axis_size("wide"), lax.axis_size("narrow")
    held, freqs, parts, _ = sigma_irr.shape
    syms, orbitals = rep_matrices.shape[:2]
    rows_y, length = star_irr.shape[1:]
    per_tile = LANES // orbitals
    per_dest = length // wide
    steps = orbitals // SUB
    tile_rows = SUB * -(-per_dest * freqs * orbitals // LANES)
    size_x, size_y = wide * star_irr.shape[0], narrow * rows_y
    rows_x = size_x // narrow

    blocks = spread_blocks(sigma_irr, orbitals, per_tile)
    vmem = pl.BlockSpec(memory_space=pltpu.VMEM)
    smem = pl.BlockSpec(memory_space=pltpu.SMEM)
    sent = pl.pallas_call(
        functools.partial(
            unfold_kernel, held, per_tile, orbitals, 1.0 / math.sqrt(size_x * size_y * length)
        ),
        out_shape=jax.ShapeDtypeStruct((wide, steps, 2, rows_y, tile_rows, LANES), jnp.float32),
        in_specs=[smem, smem, vmem, vmem, vmem],
        out_specs=vmem,
        scratch_shapes=[
            pltpu.VMEM((2, rows_y * length, orbitals, LANES), jnp.float32),
            pltpu.VMEM((syms, per_tile * orbitals + LANES - orbitals, LANES), jnp.float32),
            pltpu.VMEM((syms, orbitals, LANES), jnp.float32),
        ],
        compiler_params=pltpu.CompilerParams(vmem_limit_bytes=56 * 1024 * 1024),
    )(star_irr, star_sym, blocks, rep_matrices, jnp.swapaxes(rep_matrices, 1, 2))

    slots = (steps, 2, rows_y, tile_rows, LANES)
    middle = (narrow, steps, rows_x, 2, rows_y, tile_rows, LANES)
    result = pl.pallas_call(
        functools.partial(exchange_kernel, orbitals),
        out_shape=jax.ShapeDtypeStruct((rows_x, size_y, per_dest, freqs, 2, orbitals, orbitals), jnp.float32),
        in_specs=[vmem],
        out_specs=vmem,
        scratch_shapes=[
            pltpu.VMEM((wide,) + slots, jnp.float32),
            pltpu.VMEM(middle, jnp.float32),
            pltpu.VMEM(middle, jnp.float32),
            pltpu.SemaphoreType.DMA((steps, wide)),
            pltpu.SemaphoreType.DMA((steps, wide)),
            pltpu.SemaphoreType.DMA((steps, narrow)),
            pltpu.SemaphoreType.DMA((steps, narrow)),
            pltpu.SemaphoreType.DMA((steps + 1,)),
        ],
        compiler_params=pltpu.CompilerParams(
            collective_id=0, has_side_effects=True, vmem_limit_bytes=56 * 1024 * 1024
        ),
    )(sent)
    return result.reshape(result.shape[:5] + (orbitals * orbitals,))


def solution(mesh):
    placed = (
        P("wide", None, None, None),
        P("wide", "narrow", None),
        P("wide", "narrow", None),
        P(),
    )
    return jax.shard_map(
        local,
        mesh=mesh,
        in_specs=placed,
        out_specs=P("narrow", None, "wide", None, None, None),
        check_vma=False,
    )
```

```python
import functools
import math

import jax
import jax.numpy as jnp
from jax import lax
from jax.experimental import pallas as pl
from jax.experimental.pallas import tpu as pltpu
from jax.sharding import PartitionSpec as P

MESH = pl.DeviceIdType.MESH
LANES = 128
SUB = 8


def twiddle(value, step, length):
    real, imag = value
    step %= length
    if step == 0:
        return value
    if 4 * step == length:
        return imag, -real
    if 2 * step == length:
        return -real, -imag
    if 8 * step == length:
        root = math.sqrt(0.5)
        return (real + imag) * root, (imag - real) * root
    if 8 * step == 3 * length:
        root = math.sqrt(0.5)
        return (imag - real) * root, -(real + imag) * root
    cosine = math.cos(2 * math.pi * step / length)
    sine = math.sin(2 * math.pi * step / length)
    return real * cosine + imag * sine, imag * cosine - real * sine


def fourier(values):
    length = len(values)
    if length == 1:
        return values
    even = fourier(values[0::2])
    odd = fourier(values[1::2])
    half = length // 2
    odd = [twiddle(odd[i], i, length) for i in range(half)]
    low = [(a[0] + b[0], a[1] + b[1]) for a, b in zip(even, odd)]
    high = [(a[0] - b[0], a[1] - b[1]) for a, b in zip(even, odd)]
    return low + high


def pack(blocks, width):
    total = width * len(blocks)
    tiles = -(-total // LANES)
    lane = lax.broadcasted_iota(jnp.int32, blocks[0].shape, 1)
    made = [None] * tiles
    for index, block in enumerate(blocks):
        tile, offset = divmod(index * width, LANES)
        moved = pltpu.roll(block, offset, 1) if offset else block
        made[tile] = moved if made[tile] is None else jnp.where(lane < offset, made[tile], moved)
        if offset + width > LANES:
            made[tile + 1] = moved
    return made


def unpack(tiles, index, width):
    tile, offset = divmod(index * width, LANES)
    block = tiles[tile]
    if offset + width > LANES:
        lane = lax.broadcasted_iota(jnp.int32, block.shape, 1)
        block = jnp.where(lane >= offset, block, tiles[tile + 1])
    return pltpu.roll(block, LANES - offset, 1) if offset else block


def halves(value):
    high = value.astype(jnp.bfloat16)
    low = (value - high.astype(jnp.float32)).astype(jnp.bfloat16)
    return high, low


def unfold_kernel(
    held, per_tile, orbitals, scale, irr_ref, sym_ref, blocks_ref, rep_ref, turned_ref, out_ref, unfolded, right_ref, left_ref
):
    wide, steps, _, _, _ = out_ref.shape
    rows_y, length = irr_ref.shape[1:]
    full = out_ref.shape[3] // SUB // rows_y
    points = rows_y * length
    lane = lax.broadcasted_iota(jnp.int32, (orbitals, LANES), 1)
    first = lane < orbitals

    def one_table(sym, carry):
        rep, turned = rep_ref[sym], turned_ref[sym]
        high = rep.astype(jnp.bfloat16).astype(jnp.float32)
        rest = jnp.zeros((orbitals, LANES - 3 * orbitals), jnp.float32)
        left_ref[sym] = jnp.concatenate([high, high, rep - high, rest], axis=1)
        before = (per_tile - 1) * orbitals
        right_ref[sym, 0:before, :] = jnp.zeros((before, LANES), jnp.float32)
        rest = jnp.zeros((orbitals, LANES - 2 * orbitals), jnp.float32)
        right_ref[sym, before : before + orbitals, :] = jnp.concatenate([turned, turned, rest], axis=1)
        right_ref[sym, before + orbitals :, :] = jnp.zeros((LANES - orbitals, LANES), jnp.float32)
        return carry

    lax.fori_loop(0, rep_ref.shape[0], one_table, 0, unroll=2)

    def one_point(k, carry):
        irr = irr_ref[0, k // length, lax.rem(k, length)]
        sym = sym_ref[0, k // length, lax.rem(k, length)]
        owner = irr // held
        row = irr - owner * held
        tile = row // per_tile
        shift = (row - tile * per_tile) * orbitals
        block = blocks_ref[owner, :, pl.ds(pl.multiple_of(tile * LANES, LANES), LANES)]
        start = pl.multiple_of((per_tile - 1) * orbitals - shift, SUB)
        weights = right_ref[sym, pl.ds(start, LANES), :]
        high, low = halves(weights)
        block_high, block_low = halves(block)
        product = jnp.dot(
            jnp.concatenate([block_high, block_low], axis=1),
            jnp.concatenate(
                [
                    jnp.concatenate([high, low], axis=1),
                    jnp.concatenate([high, jnp.zeros_like(low)], axis=1),
                ],
                axis=0,
            ),
            preferred_element_type=jnp.float32,
        )
        product = product[:, :LANES] + product[:, LANES:]
        parts = []
        for c in range(2):
            base = 2 * c * orbitals
            parts.append(
                jnp.where(first, product[base : base + orbitals], product[base + orbitals : base + 2 * orbitals])
            )
        half = jnp.concatenate(parts, axis=1)
        half_high = half.astype(jnp.bfloat16).astype(jnp.float32)
        stacked = jnp.concatenate(
            [half_high, half - half_high, half_high, jnp.zeros((LANES - 3 * orbitals, 2 * LANES), jnp.float32)],
            axis=0,
        )
        turned = jnp.dot(
            left_ref[sym].astype(jnp.bfloat16),
            stacked.astype(jnp.bfloat16),
            preferred_element_type=jnp.float32,
        )
        unfolded[0, k] = turned[:, :LANES]
        unfolded[1, k] = turned[:, LANES:]
        return carry

    lax.fori_loop(0, points, one_point, 0, unroll=4)

    per_dest = length // wide

    def one_transform(y, step, carry):
        rows = pl.ds(pl.multiple_of(step * SUB, SUB), SUB)
        values = [(unfolded[0, y * length + z, rows, :], unfolded[1, y * length + z, rows, :]) for z in range(length)]
        result = fourier(values)
        for dest in range(wide):
            for c in range(2):
                made = pack([result[dest * per_dest + i][c] * scale for i in range(per_dest)], 2 * orbitals)
                for j, tile in enumerate(made):
                    at = (y * full + j if j < full else rows_y * full) * SUB
                    if j == full and y:
                        shared = out_ref[dest, step, c, at : at + SUB, :]
                        where = lax.broadcasted_iota(jnp.int32, tile.shape, 1)
                        tile = jnp.where(where < LANES // 2, shared, pltpu.roll(tile, LANES // 2, 1))
                    out_ref[dest, step, c, at : at + SUB, :] = tile
        return carry

    for y in range(rows_y):
        lax.fori_loop(0, steps, functools.partial(one_transform, y), 0)


def exchange_kernel(
    orbitals, y_ref, out_ref, from_wide, to_narrow, from_narrow, send_wide, recv_wide, send_narrow, recv_narrow, own
):
    wide, steps, _, tile_rows, _ = y_ref.shape
    narrow, _, rows_x = to_narrow.shape[:3]
    rows_y = out_ref.shape[1] // narrow
    tiles = tile_rows // SUB
    full = tiles // rows_y
    lines = full + tiles % rows_y
    me_wide = lax.axis_index("wide")
    me_narrow = lax.axis_index("narrow")

    barrier = pltpu.get_barrier_semaphore()
    for i in range(1, wide):
        pl.semaphore_signal(barrier, inc=1, device_id=(lax.rem(me_wide + i, wide), me_narrow), device_id_type=MESH)
    for i in range(1, narrow):
        pl.semaphore_signal(barrier, inc=1, device_id=(me_wide, lax.rem(me_narrow + i, narrow)), device_id_type=MESH)
    pl.semaphore_wait(barrier, wide + narrow - 2)

    def wide_copy(step, i):
        peer = lax.rem(me_wide + i, wide)
        return pltpu.make_async_remote_copy(
            src_ref=y_ref.at[peer, step],
            dst_ref=from_wide.at[me_wide, step],
            send_sem=send_wide.at[step, i],
            recv_sem=recv_wide.at[step, i],
            device_id=(peer, me_narrow),
            device_id_type=MESH,
        )

    def narrow_copy(step, i):
        peer = lax.rem(me_narrow + i, narrow)
        return pltpu.make_async_remote_copy(
            src_ref=to_narrow.at[peer, step],
            dst_ref=from_narrow.at[me_narrow, step],
            send_sem=send_narrow.at[step, i],
            recv_sem=recv_narrow.at[step, i],
            device_id=(me_wide, peer),
            device_id_type=MESH,
        )

    for step in range(steps):
        for i in range(1, wide):
            wide_copy(step, i).start()
    own_copy = pltpu.make_async_copy(y_ref.at[me_wide], from_wide.at[me_wide], own.at[steps])
    own_copy.start()
    own_copy.wait()

    def finish(step):
        for i in range(1, narrow):
            narrow_copy(step, i).wait_recv()
        rows = slice(step * SUB, (step + 1) * SUB)

        def one(x, carry):
            made = []
            for j in range(lines):
                values = []
                for n in range(narrow):
                    for y in range(rows_y):
                        at = (y * full + j if j < full else rows_y * full) * SUB
                        pair = [from_narrow[n, step, x, c, at : at + SUB, :] for c in range(2)]
                        if j == full and y:
                            pair = [pltpu.roll(value, LANES // 2, 1) for value in pair]
                        values.append(tuple(pair))
                made.append(fourier(values))
            for y in range(narrow * rows_y):
                for c in range(2):
                    line = [made[j][y][c] for j in range(lines)]
                    for z in range(out_ref.shape[2]):
                        for f in range(2):
                            block = unpack(line, 2 * z + f, orbitals)
                            out_ref[x, y, z, f, c, rows, :] = block[:, :orbitals]
            return carry

        lax.fori_loop(0, rows_x, one, 0)

    for step in range(steps):
        for i in range(1, wide):
            wide_copy(step, i).wait_recv()

        def one(at, carry):
            rows = pl.ds(pl.multiple_of(at * SUB, SUB), SUB)
            values = [(from_wide[w, step, 0, rows, :], from_wide[w, step, 1, rows, :]) for w in range(wide)]
            for x, pair in enumerate(fourier(values)):
                for c in range(2):
                    to_narrow[x // rows_x, step, x % rows_x, c, rows, :] = pair[c]
            return carry

        lax.fori_loop(0, tiles, one, 0)
        for i in range(1, narrow):
            narrow_copy(step, i).start()
        mine = pltpu.make_async_copy(to_narrow.at[me_narrow, step], from_narrow.at[me_narrow, step], own.at[step])
        mine.start()
        mine.wait()
        if step:
            finish(step - 1)
    finish(steps - 1)
    for step in range(steps):
        for i in range(1, wide):
            wide_copy(step, i).wait_send()
        for i in range(1, narrow):
            narrow_copy(step, i).wait_send()


def gather_kernel(own_ref, out_ref, send, recv, local_sem):
    depth = out_ref.shape[0] // 2
    wide, narrow = lax.axis_index("wide"), lax.axis_index("narrow")
    z, x = wide // 2, lax.rem(wide, 2)
    y, core = narrow // 2, lax.rem(narrow, 2)
    other_x = z * 2 + 1 - x
    other_y = (1 - y) * 2 + core
    x_peer, y_peer = (other_x, narrow), (wide, other_y)
    core_peer = (wide, y * 2 + 1 - core)
    z_peers = [(lax.rem(z + i, depth) * 2 + x, narrow) for i in range(1, depth)]

    barrier = pltpu.get_barrier_semaphore()
    for peer in z_peers + [x_peer, y_peer, core_peer]:
        pl.semaphore_signal(barrier, inc=1, device_id=peer, device_id_type=MESH)
    pl.semaphore_wait(barrier, depth + 2)

    mine = pltpu.make_async_copy(own_ref, out_ref.at[wide, narrow], local_sem)
    mine.start()
    copies = {}

    def push(name, peer, block):
        at = len(copies)
        source = own_ref if block is None else out_ref.at[block]
        target = (wide, narrow) if block is None else block
        copies[name] = pltpu.make_async_remote_copy(
            src_ref=source,
            dst_ref=out_ref.at[target],
            send_sem=send.at[at],
            recv_sem=recv.at[at],
            device_id=peer,
            device_id_type=MESH,
        )
        copies[name].start()

    def held(j, other_wide, other_narrow):
        source = lax.rem(z + depth - j, depth) * 2 + (1 - x if other_wide else x)
        return source, other_y if other_narrow else narrow

    push("x0", x_peer, None)
    push("y0", y_peer, None)
    for i in range(1, depth):
        push(f"z{i}", z_peers[i - 1], None)
    push("c0", core_peer, None)

    def arrived_z(j):
        copies[f"z{j}"].wait_recv()
        push(f"x{j}", x_peer, held(j, False, False))
        push(f"y{j}", y_peer, held(j, False, False))
        push(f"c{j}", core_peer, held(j, False, False))

    def arrived_xy(j):
        copies[f"x{j}"].wait_recv()
        if 2 * j < depth:
            push(f"yx{j}", y_peer, held(j, True, False))
        push(f"cx{j}", core_peer, held(j, True, False))
        copies[f"y{j}"].wait_recv()
        if 2 * j >= depth:
            push(f"xy{j}", x_peer, held(j, False, True))
        push(f"cy{j}", core_peer, held(j, False, True))

    for j in range(depth):
        if j + 1 < depth:
            arrived_z(j + 1)
        arrived_xy(j)
    for j in range(depth):
        copies[f"yx{j}" if 2 * j < depth else f"xy{j}"].wait_recv()
        push(f"cxy{j}", core_peer, held(j, True, True))
    for name, copy in copies.items():
        if name[0] == "c":
            copy.wait_recv()
    for copy in copies.values():
        copy.wait_send()
    mine.wait()


def gather_blocks(own):
    wide, narrow = lax.axis_size("wide"), lax.axis_size("narrow")
    rows, columns = own.shape
    count = wide * narrow - 1
    vmem = pl.BlockSpec(memory_space=pltpu.VMEM)
    every = pl.pallas_call(
        gather_kernel,
        out_shape=jax.ShapeDtypeStruct((wide, narrow, rows, columns), jnp.float32),
        in_specs=[vmem],
        out_specs=vmem,
        scratch_shapes=[
            pltpu.SemaphoreType.DMA((count,)),
            pltpu.SemaphoreType.DMA((count,)),
            pltpu.SemaphoreType.DMA,
        ],
        compiler_params=pltpu.CompilerParams(
            collective_id=1, has_side_effects=True, vmem_limit_bytes=32 * 1024 * 1024
        ),
    )(own)
    return every.reshape(wide, narrow * rows, columns)


def spread_blocks(sigma_irr, orbitals, per_tile):
    held, freqs, parts, _ = sigma_irr.shape
    narrow = lax.axis_size("narrow")
    tiles = -(-held // per_tile)
    share = narrow // (freqs * parts)
    if share and orbitals // share % SUB == 0:
        axes = ("wide", "narrow")
        index = lax.axis_index("narrow")
        which, piece = index // share, index % share
        part, freq = which // freqs, which % freqs
        width = orbitals * orbitals // share
        own = lax.dynamic_slice(sigma_irr, (0, freq, part, piece * width), (held, 1, 1, width))
    else:
        axes = "wide"
        own = jnp.swapaxes(sigma_irr, 1, 2)
    own = own.reshape(held, -1, orbitals).transpose(1, 0, 2)
    rows = own.shape[0]
    own = jnp.pad(own, ((0, 0), (0, tiles * per_tile - held), (0, 0)))
    own = own.reshape(rows, tiles, per_tile * orbitals)
    own = jnp.pad(own, ((0, 0), (0, 0), (0, LANES - per_tile * orbitals)))
    own = own.reshape(rows, tiles * LANES)
    if (lax.axis_size("wide"), narrow) == (8, 4) and len(axes) == 2:
        return gather_blocks(own)
    every = lax.all_gather(own, axes, axis=0, tiled=True)
    return every.reshape(lax.axis_size("wide"), freqs * parts * orbitals, tiles * LANES)


def local(sigma_irr, star_irr, star_sym, rep_matrices):
    wide, narrow = lax.axis_size("wide"), lax.axis_size("narrow")
    held, freqs, parts, _ = sigma_irr.shape
    syms, orbitals = rep_matrices.shape[:2]
    rows_y, length = star_irr.shape[1:]
    per_tile = LANES // orbitals
    per_dest = length // wide
    steps = orbitals // SUB
    used = per_dest * freqs * orbitals
    if rows_y == 2 and used % LANES == LANES // 2:
        tile_rows = SUB * (2 * used // LANES)
    else:
        tile_rows = SUB * rows_y * -(-used // LANES)
    size_x, size_y = wide * star_irr.shape[0], narrow * rows_y
    rows_x = size_x // narrow

    blocks = spread_blocks(sigma_irr, orbitals, per_tile)
    vmem = pl.BlockSpec(memory_space=pltpu.VMEM)
    smem = pl.BlockSpec(memory_space=pltpu.SMEM)
    sent = pl.pallas_call(
        functools.partial(
            unfold_kernel, held, per_tile, orbitals, 1.0 / math.sqrt(size_x * size_y * length)
        ),
        out_shape=jax.ShapeDtypeStruct((wide, steps, 2, tile_rows, LANES), jnp.float32),
        in_specs=[smem, smem, vmem, vmem, vmem],
        out_specs=vmem,
        scratch_shapes=[
            pltpu.VMEM((2, rows_y * length, orbitals, LANES), jnp.float32),
            pltpu.VMEM((syms, per_tile * orbitals + LANES - orbitals, LANES), jnp.float32),
            pltpu.VMEM((syms, orbitals, LANES), jnp.float32),
        ],
        compiler_params=pltpu.CompilerParams(vmem_limit_bytes=56 * 1024 * 1024),
    )(star_irr, star_sym, blocks, rep_matrices, jnp.swapaxes(rep_matrices, 1, 2))

    slots = (steps, 2, tile_rows, LANES)
    middle = (narrow, steps, rows_x, 2, tile_rows, LANES)
    result = pl.pallas_call(
        functools.partial(exchange_kernel, orbitals),
        out_shape=jax.ShapeDtypeStruct((rows_x, size_y, per_dest, freqs, 2, orbitals, orbitals), jnp.float32),
        in_specs=[vmem],
        out_specs=vmem,
        scratch_shapes=[
            pltpu.VMEM((wide,) + slots, jnp.float32),
            pltpu.VMEM(middle, jnp.float32),
            pltpu.VMEM(middle, jnp.float32),
            pltpu.SemaphoreType.DMA((steps, wide)),
            pltpu.SemaphoreType.DMA((steps, wide)),
            pltpu.SemaphoreType.DMA((steps, narrow)),
            pltpu.SemaphoreType.DMA((steps, narrow)),
            pltpu.SemaphoreType.DMA((steps + 1,)),
        ],
        compiler_params=pltpu.CompilerParams(
            collective_id=0, has_side_effects=True, vmem_limit_bytes=56 * 1024 * 1024
        ),
    )(sent)
    return result.reshape(result.shape[:5] + (orbitals * orbitals,))


def solution(mesh):
    placed = (
        P("wide", None, None, None),
        P("wide", "narrow", None),
        P("wide", "narrow", None),
        P(),
    )
    return jax.shard_map(
        local,
        mesh=mesh,
        in_specs=placed,
        out_specs=P("narrow", None, "wide", None, None, None),
        check_vma=False,
    )
```

```python
import functools
import math

import jax
import jax.numpy as jnp
from jax import lax
from jax.experimental import pallas as pl
from jax.experimental.pallas import tpu as pltpu
from jax.sharding import PartitionSpec as P

MESH = pl.DeviceIdType.MESH
LANES = 128
SUB = 8


def twiddle(value, step, length):
    real, imag = value
    step %= length
    if step == 0:
        return value
    if 4 * step == length:
        return imag, -real
    if 2 * step == length:
        return -real, -imag
    if 8 * step == length:
        root = math.sqrt(0.5)
        return (real + imag) * root, (imag - real) * root
    if 8 * step == 3 * length:
        root = math.sqrt(0.5)
        return (imag - real) * root, -(real + imag) * root
    cosine = math.cos(2 * math.pi * step / length)
    sine = math.sin(2 * math.pi * step / length)
    return real * cosine + imag * sine, imag * cosine - real * sine


def fourier(values):
    length = len(values)
    if length == 1:
        return values
    even = fourier(values[0::2])
    odd = fourier(values[1::2])
    half = length // 2
    odd = [twiddle(odd[i], i, length) for i in range(half)]
    low = [(a[0] + b[0], a[1] + b[1]) for a, b in zip(even, odd)]
    high = [(a[0] - b[0], a[1] - b[1]) for a, b in zip(even, odd)]
    return low + high


def pack(blocks, width):
    total = width * len(blocks)
    tiles = -(-total // LANES)
    lane = lax.broadcasted_iota(jnp.int32, blocks[0].shape, 1)
    made = [None] * tiles
    for index, block in enumerate(blocks):
        tile, offset = divmod(index * width, LANES)
        moved = pltpu.roll(block, offset, 1) if offset else block
        made[tile] = moved if made[tile] is None else jnp.where(lane < offset, made[tile], moved)
        if offset + width > LANES:
            made[tile + 1] = moved
    return made


def unpack(tiles, index, width):
    tile, offset = divmod(index * width, LANES)
    block = tiles[tile]
    if offset + width > LANES:
        lane = lax.broadcasted_iota(jnp.int32, block.shape, 1)
        block = jnp.where(lane >= offset, block, tiles[tile + 1])
    return pltpu.roll(block, LANES - offset, 1) if offset else block


def halves(value):
    high = value.astype(jnp.bfloat16)
    low = (value - high.astype(jnp.float32)).astype(jnp.bfloat16)
    return high, low


def unfold_kernel(
    held, per_tile, orbitals, scale, irr_ref, sym_ref, blocks_ref, rep_ref, turned_ref, out_ref, unfolded, right_ref, left_ref
):
    wide, steps, _, _, _ = out_ref.shape
    rows_y, length = irr_ref.shape[1:]
    full = out_ref.shape[3] // SUB // rows_y
    points = rows_y * length
    lane = lax.broadcasted_iota(jnp.int32, (orbitals, LANES), 1)
    first = lane < orbitals

    def one_table(sym, carry):
        rep, turned = rep_ref[sym], turned_ref[sym]
        high = rep.astype(jnp.bfloat16).astype(jnp.float32)
        rest = jnp.zeros((orbitals, LANES - 3 * orbitals), jnp.float32)
        left_ref[sym] = jnp.concatenate([high, high, rep - high, rest], axis=1)
        before = (per_tile - 1) * orbitals
        right_ref[sym, 0:before, :] = jnp.zeros((before, LANES), jnp.float32)
        rest = jnp.zeros((orbitals, LANES - 2 * orbitals), jnp.float32)
        right_ref[sym, before : before + orbitals, :] = jnp.concatenate([turned, turned, rest], axis=1)
        right_ref[sym, before + orbitals :, :] = jnp.zeros((LANES - orbitals, LANES), jnp.float32)
        return carry

    lax.fori_loop(0, rep_ref.shape[0], one_table, 0, unroll=2)

    def one_point(k, carry):
        irr = irr_ref[0, k // length, lax.rem(k, length)]
        sym = sym_ref[0, k // length, lax.rem(k, length)]
        owner = irr // held
        row = irr - owner * held
        tile = row // per_tile
        shift = (row - tile * per_tile) * orbitals
        block = blocks_ref[owner, :, pl.ds(pl.multiple_of(tile * LANES, LANES), LANES)]
        start = pl.multiple_of((per_tile - 1) * orbitals - shift, SUB)
        weights = right_ref[sym, pl.ds(start, LANES), :]
        high, low = halves(weights)
        block_high, block_low = halves(block)
        product = jnp.dot(
            jnp.concatenate([block_high, block_low], axis=1),
            jnp.concatenate(
                [
                    jnp.concatenate([high, low], axis=1),
                    jnp.concatenate([high, jnp.zeros_like(low)], axis=1),
                ],
                axis=0,
            ),
            preferred_element_type=jnp.float32,
        )
        product = product[:, :LANES] + product[:, LANES:]
        parts = []
        for c in range(2):
            base = 2 * c * orbitals
            parts.append(
                jnp.where(first, product[base : base + orbitals], product[base + orbitals : base + 2 * orbitals])
            )
        half = jnp.concatenate(parts, axis=1)
        half_high = half.astype(jnp.bfloat16).astype(jnp.float32)
        stacked = jnp.concatenate(
            [half_high, half - half_high, half_high, jnp.zeros((LANES - 3 * orbitals, 2 * LANES), jnp.float32)],
            axis=0,
        )
        turned = jnp.dot(
            left_ref[sym].astype(jnp.bfloat16),
            stacked.astype(jnp.bfloat16),
            preferred_element_type=jnp.float32,
        )
        unfolded[0, k] = turned[:, :LANES]
        unfolded[1, k] = turned[:, LANES:]
        return carry

    lax.fori_loop(0, points, one_point, 0, unroll=8)

    per_dest = length // wide

    def one_transform(y, step, carry):
        rows = pl.ds(pl.multiple_of(step * SUB, SUB), SUB)
        values = [(unfolded[0, y * length + z, rows, :], unfolded[1, y * length + z, rows, :]) for z in range(length)]
        result = fourier(values)
        for dest in range(wide):
            for c in range(2):
                made = pack([result[dest * per_dest + i][c] * scale for i in range(per_dest)], 2 * orbitals)
                for j, tile in enumerate(made):
                    at = (y * full + j if j < full else rows_y * full) * SUB
                    if j == full and y:
                        shared = out_ref[dest, step, c, at : at + SUB, :]
                        where = lax.broadcasted_iota(jnp.int32, tile.shape, 1)
                        tile = jnp.where(where < LANES // 2, shared, pltpu.roll(tile, LANES // 2, 1))
                    out_ref[dest, step, c, at : at + SUB, :] = tile
        return carry

    for y in range(rows_y):
        lax.fori_loop(0, steps, functools.partial(one_transform, y), 0)


def exchange_kernel(
    orbitals, y_ref, out_ref, from_wide, to_narrow, from_narrow, send_wide, recv_wide, send_narrow, recv_narrow, own
):
    wide, steps, _, tile_rows, _ = y_ref.shape
    narrow, _, rows_x = to_narrow.shape[:3]
    rows_y = out_ref.shape[1] // narrow
    tiles = tile_rows // SUB
    full = tiles // rows_y
    lines = full + tiles % rows_y
    me_wide = lax.axis_index("wide")
    me_narrow = lax.axis_index("narrow")

    barrier = pltpu.get_barrier_semaphore()
    for i in range(1, wide):
        pl.semaphore_signal(barrier, inc=1, device_id=(lax.rem(me_wide + i, wide), me_narrow), device_id_type=MESH)
    for i in range(1, narrow):
        pl.semaphore_signal(barrier, inc=1, device_id=(me_wide, lax.rem(me_narrow + i, narrow)), device_id_type=MESH)
    pl.semaphore_wait(barrier, wide + narrow - 2)

    def wide_copy(step, i):
        peer = lax.rem(me_wide + i, wide)
        return pltpu.make_async_remote_copy(
            src_ref=y_ref.at[peer, step],
            dst_ref=from_wide.at[me_wide, step],
            send_sem=send_wide.at[step, i],
            recv_sem=recv_wide.at[step, i],
            device_id=(peer, me_narrow),
            device_id_type=MESH,
        )

    def narrow_copy(step, i):
        peer = lax.rem(me_narrow + i, narrow)
        return pltpu.make_async_remote_copy(
            src_ref=to_narrow.at[peer, step],
            dst_ref=from_narrow.at[me_narrow, step],
            send_sem=send_narrow.at[step, i],
            recv_sem=recv_narrow.at[step, i],
            device_id=(me_wide, peer),
            device_id_type=MESH,
        )

    for step in range(steps):
        for i in range(1, wide):
            wide_copy(step, i).start()
    own_copy = pltpu.make_async_copy(y_ref.at[me_wide], from_wide.at[me_wide], own.at[steps])
    own_copy.start()
    own_copy.wait()

    def finish(step):
        for i in range(1, narrow):
            narrow_copy(step, i).wait_recv()
        rows = slice(step * SUB, (step + 1) * SUB)

        def one(x, carry):
            made = []
            for j in range(lines):
                values = []
                for n in range(narrow):
                    for y in range(rows_y):
                        at = (y * full + j if j < full else rows_y * full) * SUB
                        pair = [from_narrow[n, step, x, c, at : at + SUB, :] for c in range(2)]
                        if j == full and y:
                            pair = [pltpu.roll(value, LANES // 2, 1) for value in pair]
                        values.append(tuple(pair))
                made.append(fourier(values))
            for y in range(narrow * rows_y):
                for c in range(2):
                    line = [made[j][y][c] for j in range(lines)]
                    for z in range(out_ref.shape[2]):
                        for f in range(2):
                            block = unpack(line, 2 * z + f, orbitals)
                            out_ref[x, y, z, f, c, rows, :] = block[:, :orbitals]
            return carry

        lax.fori_loop(0, rows_x, one, 0)

    for step in range(steps):
        for i in range(1, wide):
            wide_copy(step, i).wait_recv()

        def one(at, carry):
            rows = pl.ds(pl.multiple_of(at * SUB, SUB), SUB)
            values = [(from_wide[w, step, 0, rows, :], from_wide[w, step, 1, rows, :]) for w in range(wide)]
            for x, pair in enumerate(fourier(values)):
                for c in range(2):
                    to_narrow[x // rows_x, step, x % rows_x, c, rows, :] = pair[c]
            return carry

        lax.fori_loop(0, tiles, one, 0)
        for i in range(1, narrow):
            narrow_copy(step, i).start()
        mine = pltpu.make_async_copy(to_narrow.at[me_narrow, step], from_narrow.at[me_narrow, step], own.at[step])
        mine.start()
        mine.wait()
        if step:
            finish(step - 1)
    finish(steps - 1)
    for step in range(steps):
        for i in range(1, wide):
            wide_copy(step, i).wait_send()
        for i in range(1, narrow):
            narrow_copy(step, i).wait_send()


def gather_kernel(own_ref, out_ref, send, recv, local_sem):
    depth = out_ref.shape[0] // 2
    wide, narrow = lax.axis_index("wide"), lax.axis_index("narrow")
    z, x = wide // 2, lax.rem(wide, 2)
    y, core = narrow // 2, lax.rem(narrow, 2)
    other_x = z * 2 + 1 - x
    other_y = (1 - y) * 2 + core
    x_peer, y_peer = (other_x, narrow), (wide, other_y)
    core_peer = (wide, y * 2 + 1 - core)
    z_peers = [(lax.rem(z + i, depth) * 2 + x, narrow) for i in range(1, depth)]

    barrier = pltpu.get_barrier_semaphore()
    for peer in z_peers + [x_peer, y_peer, core_peer]:
        pl.semaphore_signal(barrier, inc=1, device_id=peer, device_id_type=MESH)
    pl.semaphore_wait(barrier, depth + 2)

    mine = pltpu.make_async_copy(own_ref, out_ref.at[wide, narrow], local_sem)
    mine.start()
    copies = {}

    def push(name, peer, block):
        at = len(copies)
        source = own_ref if block is None else out_ref.at[block]
        target = (wide, narrow) if block is None else block
        copies[name] = pltpu.make_async_remote_copy(
            src_ref=source,
            dst_ref=out_ref.at[target],
            send_sem=send.at[at],
            recv_sem=recv.at[at],
            device_id=peer,
            device_id_type=MESH,
        )
        copies[name].start()

    def held(j, other_wide, other_narrow):
        source = lax.rem(z + depth - j, depth) * 2 + (1 - x if other_wide else x)
        return source, other_y if other_narrow else narrow

    push("x0", x_peer, None)
    push("y0", y_peer, None)
    for i in range(1, depth):
        push(f"z{i}", z_peers[i - 1], None)
    push("c0", core_peer, None)

    def arrived_z(j):
        copies[f"z{j}"].wait_recv()
        push(f"x{j}", x_peer, held(j, False, False))
        push(f"y{j}", y_peer, held(j, False, False))
        push(f"c{j}", core_peer, held(j, False, False))

    def arrived_xy(j):
        copies[f"x{j}"].wait_recv()
        if 2 * j < depth:
            push(f"yx{j}", y_peer, held(j, True, False))
        push(f"cx{j}", core_peer, held(j, True, False))
        copies[f"y{j}"].wait_recv()
        if 2 * j >= depth:
            push(f"xy{j}", x_peer, held(j, False, True))
        push(f"cy{j}", core_peer, held(j, False, True))

    for j in range(depth):
        if j + 1 < depth:
            arrived_z(j + 1)
        arrived_xy(j)
    for j in range(depth):
        copies[f"yx{j}" if 2 * j < depth else f"xy{j}"].wait_recv()
        push(f"cxy{j}", core_peer, held(j, True, True))
    for name, copy in copies.items():
        if name[0] == "c":
            copy.wait_recv()
    for copy in copies.values():
        copy.wait_send()
    mine.wait()


def gather_blocks(own):
    wide, narrow = lax.axis_size("wide"), lax.axis_size("narrow")
    rows, columns = own.shape
    count = wide * narrow - 1
    vmem = pl.BlockSpec(memory_space=pltpu.VMEM)
    every = pl.pallas_call(
        gather_kernel,
        out_shape=jax.ShapeDtypeStruct((wide, narrow, rows, columns), jnp.float32),
        in_specs=[vmem],
        out_specs=pl.BlockSpec(memory_space=pl.ANY),
        scratch_shapes=[
            pltpu.SemaphoreType.DMA((count,)),
            pltpu.SemaphoreType.DMA((count,)),
            pltpu.SemaphoreType.DMA,
        ],
        compiler_params=pltpu.CompilerParams(
            collective_id=1, has_side_effects=True, vmem_limit_bytes=32 * 1024 * 1024
        ),
    )(own)
    return every.reshape(wide, narrow * rows, columns)


def spread_blocks(sigma_irr, orbitals, per_tile):
    held, freqs, parts, _ = sigma_irr.shape
    narrow = lax.axis_size("narrow")
    tiles = -(-held // per_tile)
    share = narrow // (freqs * parts)
    if share and orbitals // share % SUB == 0:
        axes = ("wide", "narrow")
        index = lax.axis_index("narrow")
        which, piece = index // share, index % share
        part, freq = which // freqs, which % freqs
        width = orbitals * orbitals // share
        own = lax.dynamic_slice(sigma_irr, (0, freq, part, piece * width), (held, 1, 1, width))
    else:
        axes = "wide"
        own = jnp.swapaxes(sigma_irr, 1, 2)
    own = own.reshape(held, -1, orbitals).transpose(1, 0, 2)
    rows = own.shape[0]
    own = jnp.pad(own, ((0, 0), (0, tiles * per_tile - held), (0, 0)))
    own = own.reshape(rows, tiles, per_tile * orbitals)
    own = jnp.pad(own, ((0, 0), (0, 0), (0, LANES - per_tile * orbitals)))
    own = own.reshape(rows, tiles * LANES)
    if (lax.axis_size("wide"), narrow) == (8, 4) and len(axes) == 2:
        return gather_blocks(own)
    every = lax.all_gather(own, axes, axis=0, tiled=True)
    return every.reshape(lax.axis_size("wide"), freqs * parts * orbitals, tiles * LANES)


def local(sigma_irr, star_irr, star_sym, rep_matrices):
    wide, narrow = lax.axis_size("wide"), lax.axis_size("narrow")
    held, freqs, parts, _ = sigma_irr.shape
    syms, orbitals = rep_matrices.shape[:2]
    rows_y, length = star_irr.shape[1:]
    per_tile = LANES // orbitals
    per_dest = length // wide
    steps = orbitals // SUB
    used = per_dest * freqs * orbitals
    if rows_y == 2 and used % LANES == LANES // 2:
        tile_rows = SUB * (2 * used // LANES)
    else:
        tile_rows = SUB * rows_y * -(-used // LANES)
    size_x, size_y = wide * star_irr.shape[0], narrow * rows_y
    rows_x = size_x // narrow

    blocks = spread_blocks(sigma_irr, orbitals, per_tile)
    vmem = pl.BlockSpec(memory_space=pltpu.VMEM)
    smem = pl.BlockSpec(memory_space=pltpu.SMEM)
    sent = pl.pallas_call(
        functools.partial(
            unfold_kernel, held, per_tile, orbitals, 1.0 / math.sqrt(size_x * size_y * length)
        ),
        out_shape=jax.ShapeDtypeStruct((wide, steps, 2, tile_rows, LANES), jnp.float32),
        in_specs=[smem, smem, vmem, vmem, vmem],
        out_specs=vmem,
        scratch_shapes=[
            pltpu.VMEM((2, rows_y * length, orbitals, LANES), jnp.float32),
            pltpu.VMEM((syms, per_tile * orbitals + LANES - orbitals, LANES), jnp.float32),
            pltpu.VMEM((syms, orbitals, LANES), jnp.float32),
        ],
        compiler_params=pltpu.CompilerParams(vmem_limit_bytes=56 * 1024 * 1024),
    )(star_irr, star_sym, blocks, rep_matrices, jnp.swapaxes(rep_matrices, 1, 2))

    slots = (steps, 2, tile_rows, LANES)
    middle = (narrow, steps, rows_x, 2, tile_rows, LANES)
    result = pl.pallas_call(
        functools.partial(exchange_kernel, orbitals),
        out_shape=jax.ShapeDtypeStruct((rows_x, size_y, per_dest, freqs, 2, orbitals, orbitals), jnp.float32),
        in_specs=[vmem],
        out_specs=vmem,
        scratch_shapes=[
            pltpu.VMEM((wide,) + slots, jnp.float32),
            pltpu.VMEM(middle, jnp.float32),
            pltpu.VMEM(middle, jnp.float32),
            pltpu.SemaphoreType.DMA((steps, wide)),
            pltpu.SemaphoreType.DMA((steps, wide)),
            pltpu.SemaphoreType.DMA((steps, narrow)),
            pltpu.SemaphoreType.DMA((steps, narrow)),
            pltpu.SemaphoreType.DMA((steps + 1,)),
        ],
        compiler_params=pltpu.CompilerParams(
            collective_id=0, has_side_effects=True, vmem_limit_bytes=56 * 1024 * 1024
        ),
    )(sent)
    return result.reshape(result.shape[:5] + (orbitals * orbitals,))


def solution(mesh):
    placed = (
        P("wide", None, None, None),
        P("wide", "narrow", None),
        P("wide", "narrow", None),
        P(),
    )
    return jax.shard_map(
        local,
        mesh=mesh,
        in_specs=placed,
        out_specs=P("narrow", None, "wide", None, None, None),
        check_vma=False,
    )
```
